32 devices in a mesh: grp: 4 (over x, core), blk: 8 (over z, y).
Axes of the slice: x: 2, y: 2, z: 4, core: 2. Of those that a mesh axis runs over, the one named last changes fastest.
Arguments:
- image_embeds: bfloat16 [8192, 1152], P(('grp', 'blk')), may hold values from -6 to 6
- text_embeds: bfloat16 [8192, 1152], P(('grp', 'blk')), may hold values from -6 to 6
- positives: int32 [32, 256], P(('grp', 'blk')), may hold values from 0 to 255, each once within a row
- logit_scale: float32 [1], replicated, may hold values from 60 to 150
- logit_bias: float32 [1], replicated, may hold values from -4 to -1
Outputs:
- image_grad: float32 [8192, 1152], P(('grp', 'blk'))
- text_grad: float32 [8192, 1152], P(('grp', 'blk'))
The draws below stay inside these ranges and needn't reach their ends.
Inputs may be any that keep to these rules, and one draw needn't show every extreme that they name: Each row of positives names every position of its block once, so each image of a block has its own matching text.
All inputs are finite; a program needn't handle non-finite values.
Results may differ from the reference program's by a relative error of at most 0.0055.
Values may be sent and summed in bfloat16 or wider, within the bound.
A program may use at most 64 MiB of HBM per device.

```python
import math
import jax
import jax.numpy as jnp
from jax import lax

D = 1152
ROWS = 256
STEPS = 4
BLOCKS = 32
TOKENS = 8192
N_GRP = 4
N_BLK = 8


def levels(rng, shape, split, low, top_value):
    level = 1.0
    for axis_at, blocks in split:
        heights = jax.random.uniform(jax.random.fold_in(jax.random.fold_in(rng, 6), axis_at), (blocks,), jnp.float32, low / len(split), top_value / len(split))
        level = level * jnp.repeat(jnp.exp(heights), shape[axis_at] // blocks).reshape((-1,) + (1,) * (len(shape) - 1 - axis_at))
    return level


def centred(stream_key, shape, scale, most, pieces=(), kind=jnp.bfloat16):
    result = scale * jax.random.normal(stream_key, shape, jnp.float32)
    if pieces:
        result = result * levels(stream_key, shape, pieces, -0.22, 0.18)
    return jnp.clip(result, -most, most).astype(kind)


def setup_inputs(seed: int = 0) -> dict:
    arg_keys = jax.random.split(jax.random.key(seed), 6)
    return {
        "image_embeds": centred(arg_keys[0], (TOKENS, D), 1.0, 6.0, ((0, 32),)),
        "text_embeds": centred(arg_keys[1], (TOKENS, D), 1.0, 6.0, ((0, 32),)),
        "positives": jax.vmap(lambda own: jax.random.permutation(own, ROWS))(jax.random.split(arg_keys[2], BLOCKS)).reshape((BLOCKS, ROWS)).astype(jnp.int32),
        "logit_scale": jnp.clip(jnp.exp(jax.random.uniform(arg_keys[3], (1,), jnp.float32, math.log(60.0), math.log(150.0))), 60.0, 150.0),
        "logit_bias": jnp.clip(jax.random.uniform(arg_keys[4], (1,), jnp.float32, -4.0, -1.0), -4.0, -1.0),
    }


def unit_rows(embeds):
    values = embeds.astype(jnp.float32)
    inverse = lax.rsqrt(lax.optimization_barrier(jnp.sum(values * values, axis=-1, keepdims=True)) + 1e-06)
    return (values, inverse, (values * inverse).astype(jnp.bfloat16))

def unit_back(values, inverse, grad_unit):
    projection = lax.optimization_barrier(jnp.sum(values * grad_unit, axis=-1, keepdims=True))
    return inverse * grad_unit - inverse * inverse * inverse * values * projection

def pair_coef(image_rows, text_rows, label_cols, scale_value, bias_value, holds_positive):
    logits = scale_value * jnp.dot(image_rows, text_rows.T, preferred_element_type=jnp.float32) + bias_value
    if holds_positive:
        columns = lax.broadcasted_iota(jnp.int32, logits.shape, 1)
        label_sign = jnp.where(columns == label_cols[:, None], 1.0, -1.0).astype(jnp.float32)
    else:
        label_sign = -1.0
    return (-label_sign * scale_value * jax.nn.sigmoid(-label_sign * logits)).astype(jnp.bfloat16)

def reference(image_embeds, text_embeds, positives, logit_scale, logit_bias):
    image_values, image_inverse, image_unit = unit_rows(image_embeds)
    text_values, text_inverse, text_unit = unit_rows(text_embeds)
    image_tiles = image_unit.reshape(N_GRP, N_BLK, ROWS, D)
    text_tiles = text_unit.reshape(N_GRP, N_BLK, ROWS, D)
    scale_value = logit_scale[0]
    bias_value = logit_bias[0]

    def image_side(block_id):
        group_id = block_id // N_BLK
        place_id = block_id % N_BLK
        image_block = image_tiles[group_id, place_id]
        labels = positives[block_id]
        accumulated = jnp.zeros((ROWS, D), jnp.float32)
        for side_index in range(2):
            partner_id = group_id if side_index == 0 else jnp.bitwise_xor(group_id, 2)
            for offset in range(STEPS):
                source = (place_id - 2 * offset) % N_BLK
                text_block = text_tiles[partner_id, source]
                coefficient = pair_coef(image_block, text_block, labels, scale_value, bias_value, side_index == 0 and offset == 0)
                accumulated = accumulated + jnp.dot(coefficient, text_block, preferred_element_type=jnp.float32)
        return accumulated

    def text_side(block_id):
        group_id = block_id // N_BLK
        place_id = block_id % N_BLK
        text_block = text_tiles[group_id, place_id]
        accumulated = jnp.zeros((ROWS, D), jnp.float32)
        for side_index in range(2):
            partner_id = group_id if side_index == 0 else jnp.bitwise_xor(group_id, 2)
            for offset in range(STEPS):
                target = (place_id + 2 * offset) % N_BLK
                image_block = image_tiles[partner_id, target]
                labels = positives[partner_id * N_BLK + target]
                coefficient = pair_coef(image_block, text_block, labels, scale_value, bias_value, side_index == 0 and offset == 0)
                accumulated = accumulated + jnp.dot(coefficient.T, image_block, preferred_element_type=jnp.float32)
        return accumulated
    block_ids = jnp.arange(N_GRP * N_BLK, dtype=jnp.int32)
    grad_image_unit = lax.map(image_side, block_ids).reshape(TOKENS, D)
    grad_text_unit = lax.map(text_side, block_ids).reshape(TOKENS, D)
    image_grad = unit_back(image_values, image_inverse, grad_image_unit)
    text_grad = unit_back(text_values, text_inverse, grad_text_unit)
    return (image_grad, text_grad)
```

```python
import functools

import jax
import jax.numpy as jnp
from jax import lax
from jax.experimental import pallas as pl
from jax.experimental.pallas import tpu as pltpu
from jax.sharding import PartitionSpec as P

STEPS = 4
CHUNKS = 4
MESH = pl.DeviceIdType.MESH


def partner(value, axis, distance):
    mask = 2**distance
    pairs = [(source, source ^ mask) for source in range(lax.axis_size(axis))]
    return lax.ppermute(value, axis, pairs)


def shifted(value, axis, steps):
    count = lax.axis_size(axis)
    pairs = [(source, (source + steps) % count) for source in range(count)]
    return lax.ppermute(value, axis, pairs)


def unit_rows(embeds):
    values = embeds.astype(jnp.float32)
    inverse = lax.rsqrt(jnp.sum(values * values, axis=-1, keepdims=True) + 1e-06)
    return (values, inverse, (values * inverse).astype(jnp.bfloat16))


def unit_back(values, inverse, grad_unit):
    projection = jnp.sum(values * grad_unit, axis=-1, keepdims=True)
    return inverse * grad_unit - inverse * inverse * inverse * values * projection


def dot_last(a, b):
    return lax.dot_general(a, b, (((1,), (1,)), ((), ())), preferred_element_type=jnp.float32)


def dot_first(a, b):
    return lax.dot_general(a, b, (((0,), (0,)), ((), ())), preferred_element_type=jnp.float32)


def window_plan(image_embeds, text_embeds, positives, logit_scale, logit_bias):
    image_values, image_inverse, image_unit = unit_rows(image_embeds)
    text_values, text_inverse, text_unit = unit_rows(text_embeds)
    scale, bias = logit_scale[0], logit_bias[0]
    rows = image_unit.shape[0]
    images = jnp.concatenate([image_unit, partner(image_unit, "grp", 1)])
    texts = [text_unit]
    for _ in range(STEPS - 1):
        texts.append(shifted(texts[-1], "blk", 2))
    image_total = jnp.zeros((2 * rows, image_unit.shape[1]), jnp.float32)
    text_parts = []
    for step in range(STEPS):
        logits = scale * dot_last(texts[step], images) + bias
        sign = jnp.full(logits.shape, -1.0, jnp.float32)
        if step == 0:
            places = lax.broadcasted_iota(jnp.int32, (rows, rows), 0)
            own = jnp.where(places == positives[0][None, :], 1.0, -1.0)
            sign = jnp.concatenate([own, sign[:, rows:]], axis=1)
        coefficient = (-sign * scale * jax.nn.sigmoid(-sign * logits)).astype(jnp.bfloat16)
        text_parts.append(
            jnp.dot(coefficient, images, preferred_element_type=jnp.float32)
        )
        image_total = image_total + dot_first(coefficient, texts[step])
    image_grad = image_total[:rows] + partner(image_total[rows:].astype(jnp.bfloat16), "grp", 1)
    text_total = text_parts[-1]
    for step in range(STEPS - 2, -1, -1):
        text_total = text_parts[step] + shifted(text_total.astype(jnp.bfloat16), "blk", -2)
    return (
        unit_back(image_values, image_inverse, image_grad),
        unit_back(text_values, text_inverse, text_total),
    )


def line_kernel(
    img_ref, txt_ref, pos_ref, scale_ref, bias_ref, img_out, txt_out,
    images, texts, coefs, parts, img_total, back, back_send, img_send, img_recv,
    i_sems, g_send, g_recv, r_send, r_recv, x_send, x_recv,
):
    rows, width = img_ref.shape
    piece = rows // CHUNKS
    last = STEPS - 1
    g = lax.axis_index("grp")
    b = lax.axis_index("blk")
    z = b // 2
    across = {"grp": g + 2 - 4 * ((g // 2) % 2)}
    scale = scale_ref[0]
    bias = bias_ref[0]

    def at(c):
        return pl.ds(pl.multiple_of(c * piece, piece), piece)

    def device(d):
        return {"blk": b + 2 * d}

    def has(d):
        return (z + d >= 0) & (z + d <= last)

    def side(d):
        return (d + 1) // 2

    def gather_copy(d, j, c):
        part = texts.at[j, at(c)]
        return pltpu.make_async_remote_copy(
            part, part, g_send.at[side(d), j, c], g_recv.at[j, c],
            device_id=device(d), device_id_type=MESH)

    def return_copy(d, j, c):
        return pltpu.make_async_remote_copy(
            back_send.at[j, at(c)], back.at[side(d), j, at(c)],
            r_send.at[side(d), j, c], r_recv.at[side(d), j, c],
            device_id=device(d), device_id_type=MESH)

    def image_copy():
        return pltpu.make_async_remote_copy(
            images.at[pl.ds(0, rows)], images.at[pl.ds(rows, rows)], i_sems.at[0], i_sems.at[1],
            device_id=across, device_id_type=MESH)

    def total_copy(c):
        return pltpu.make_async_remote_copy(
            img_send.at[at(c)], img_recv.at[at(c)], x_send.at[c], x_recv.at[c],
            device_id=across, device_id_type=MESH)

    barrier = pltpu.get_barrier_semaphore()
    pl.semaphore_signal(barrier, inc=1, device_id=across, device_id_type=MESH)
    for d in (1, -1):
        @pl.when(has(d))
        def _():
            pl.semaphore_signal(barrier, inc=1, device_id=device(d), device_id_type=MESH)

    @pl.loop(0, CHUNKS)
    def _(c):
        texts[z, at(c)] = unit_rows(txt_ref[at(c)])[2]

    pl.semaphore_wait(barrier, 3 - z // last - (last - z) // last)

    @pl.loop(0, CHUNKS)
    def _(c):
        for d in (1, -1):
            @pl.when(has(d))
            def _():
                gather_copy(d, z, c).start()

    @pl.loop(0, CHUNKS)
    def _(c):
        images[at(c)] = unit_rows(img_ref[at(c)])[2]

    image_copy().start()

    own_images = images[pl.ds(0, rows)]
    own_texts = texts[z]
    logits = scale * dot_last(own_texts, own_images) + bias
    places = lax.broadcasted_iota(jnp.int32, logits.shape, 0)
    sign = jnp.where(places == pos_ref[...], 1.0, -1.0).astype(jnp.float32)
    coefficient = (-sign * scale * jax.nn.sigmoid(-sign * logits)).astype(jnp.bfloat16)
    parts[z] = jnp.dot(coefficient, own_images, preferred_element_type=jnp.float32)
    img_total[pl.ds(0, rows)] = dot_first(coefficient, own_texts)

    def arrive(t, c):
        for d in (1, -1):
            j = z - d * (t + 1)

            @pl.when((j >= 0) & (j <= last))
            def _():
                gather_copy(d, j, c).wait_recv()

                @pl.when(has(d))
                def _():
                    gather_copy(d, j, c).start()

    def meet(t, c):
        @pl.loop(0, 2)
        def _(q):
            j = z + (2 * q - 1) * (t + 1)

            @pl.when((j >= 0) & (j <= last))
            def _():
                both = images[...]
                logits = scale * dot_last(texts[j, at(c)], both) + bias
                coefficient = (scale * jax.nn.sigmoid(logits)).astype(jnp.bfloat16)
                coefs[j, at(c)] = coefficient
                parts[j, at(c)] = jnp.dot(coefficient, both, preferred_element_type=jnp.float32)

    def give_back(t, c):
        for d, j in ((-1, last - t), (1, t)):
            @pl.when((j - z) * d > 0)
            def _():
                @pl.when(has(-d))
                def _():
                    return_copy(d, j, c).wait_recv()
                    parts[j, at(c)] += back[side(d), j, at(c)].astype(jnp.float32)

                back_send[j, at(c)] = parts[j, at(c)].astype(jnp.bfloat16)
                return_copy(d, j, c).start()

    def add_images(j):
        img_total[...] += dot_first(coefs[j], texts[j])

    @pl.loop(0, CHUNKS)
    def _(c):
        arrive(0, c)

    image_copy().wait_recv()
    their_images = images[pl.ds(rows, rows)]
    own_texts = texts[z]
    logits = scale * dot_last(own_texts, their_images) + bias
    coefficient = (scale * jax.nn.sigmoid(logits)).astype(jnp.bfloat16)
    parts[z] += jnp.dot(coefficient, their_images, preferred_element_type=jnp.float32)
    img_total[pl.ds(rows, rows)] = dot_first(coefficient, own_texts)

    @pl.loop(0, CHUNKS)
    def _(c):
        meet(0, c)
        give_back(1, c)
        arrive(1, c)
        meet(1, c)

    @pl.loop(0, CHUNKS)
    def _(c):
        give_back(2, c)
        arrive(2, c)
        meet(2, c)

        @pl.when((c - z) * (c - z) % 9 > 0)
        def _():
            add_images(c)

    @pl.loop(0, 2)
    def _(q):
        @pl.when(z == last * q)
        def _():
            add_images(last - last * q)

    @pl.loop(0, CHUNKS)
    def _(c):
        img_send[at(c)] = img_total[pl.ds(pl.multiple_of(rows + c * piece, piece), piece)].astype(
            jnp.bfloat16
        )
        total_copy(c).start()

    @pl.loop(0, CHUNKS)
    def _(c):
        give_back(3, c)

    @pl.loop(0, CHUNKS)
    def _(c):
        for d in (1, -1):
            @pl.when(has(-d))
            def _():
                return_copy(d, z, c).wait_recv()
                parts[z, at(c)] += back[side(d), z, at(c)].astype(jnp.float32)

        values, inverse, _ = unit_rows(txt_ref[at(c)])
        txt_out[at(c)] = unit_back(values, inverse, parts[z, at(c)])

    @pl.loop(0, CHUNKS)
    def _(c):
        total_copy(c).wait_recv()
        values, inverse, _ = unit_rows(img_ref[at(c)])
        total = img_total[at(c)] + img_recv[at(c)].astype(jnp.float32)
        img_out[at(c)] = unit_back(values, inverse, total)

    image_copy().wait_send()

    @pl.loop(0, CHUNKS)
    def _(c):
        total_copy(c).wait_send()

        @pl.loop(0, STEPS)
        def _(j):
            for d in (1, -1):
                @pl.when(((z - j) * d >= 0) & has(d))
                def _():
                    gather_copy(d, j, c).wait_send()

                @pl.when((j - z) * d > 0)
                def _():
                    return_copy(d, j, c).wait_send()


def line_plan(image_embeds, text_embeds, positives, logit_scale, logit_bias):
    rows, width = image_embeds.shape
    vmem = pl.BlockSpec(memory_space=pltpu.VMEM)
    smem = pl.BlockSpec(memory_space=pltpu.SMEM)
    grad = jax.ShapeDtypeStruct((rows, width), jnp.float32)
    dma = pltpu.SemaphoreType.DMA
    half = functools.partial(pltpu.VMEM, dtype=jnp.bfloat16)
    full = functools.partial(pltpu.VMEM, dtype=jnp.float32)
    return pl.pallas_call(
        line_kernel,
        out_shape=(grad, grad),
        in_specs=[vmem, vmem, vmem, smem, smem],
        out_specs=(vmem, vmem),
        scratch_shapes=[
            half((2 * rows, width)),
            half((STEPS, rows, width)),
            half((STEPS, rows, 2 * rows)),
            full((STEPS, rows, width)),
            full((2 * rows, width)),
            half((2, STEPS, rows, width)),
            half((STEPS, rows, width)),
            half((rows, width)),
            half((rows, width)),
            dma((2,)),
            dma((2, STEPS, CHUNKS)),
            dma((STEPS, CHUNKS)),
            dma((2, STEPS, CHUNKS)),
            dma((2, STEPS, CHUNKS)),
            dma((CHUNKS,)),
            dma((CHUNKS,)),
        ],
        compiler_params=pltpu.CompilerParams(
            collective_id=0, has_side_effects=True, vmem_limit_bytes=48 * 2**20
        ),
        cost_estimate=pl.CostEstimate(
            flops=48 * rows * rows * width, bytes_accessed=12 * rows * width, transcendentals=0
        ),
    )(image_embeds, text_embeds, positives, logit_scale, logit_bias)


def solution(mesh):
    whole_line = mesh.shape["blk"] == 2 * STEPS
    return jax.shard_map(
        line_plan if whole_line else window_plan,
        mesh=mesh,
        in_specs=(
            P(("grp", "blk"), None),
            P(("grp", "blk"), None),
            P(("grp", "blk"), None),
            P(),
            P(),
        ),
        out_specs=(P(("grp", "blk"), None), P(("grp", "blk"), None)),
        check_vma=False,
    )
```

```python
import functools

import jax
import jax.numpy as jnp
from jax import lax
from jax.experimental import pallas as pl
from jax.experimental.pallas import tpu as pltpu
from jax.sharding import PartitionSpec as P

STEPS = 4
CHUNKS = 8
AHEAD = 2
LAG = 1
HOLD = 4
MESH = pl.DeviceIdType.MESH


def partner(value, axis, distance):
    mask = 2**distance
    pairs = [(source, source ^ mask) for source in range(lax.axis_size(axis))]
    return lax.ppermute(value, axis, pairs)


def shifted(value, axis, steps):
    count = lax.axis_size(axis)
    pairs = [(source, (source + steps) % count) for source in range(count)]
    return lax.ppermute(value, axis, pairs)


def unit_rows(embeds):
    values = embeds.astype(jnp.float32)
    inverse = lax.rsqrt(jnp.sum(values * values, axis=-1, keepdims=True) + 1e-06)
    return (values, inverse, (values * inverse).astype(jnp.bfloat16))


def unit_back(values, inverse, grad_unit):
    projection = jnp.sum(values * grad_unit, axis=-1, keepdims=True)
    return inverse * grad_unit - inverse * inverse * inverse * values * projection


def dot_last(a, b):
    return lax.dot_general(a, b, (((1,), (1,)), ((), ())), preferred_element_type=jnp.float32)


def dot_first(a, b):
    return lax.dot_general(a, b, (((0,), (0,)), ((), ())), preferred_element_type=jnp.float32)


def window_plan(image_embeds, text_embeds, positives, logit_scale, logit_bias):
    image_values, image_inverse, image_unit = unit_rows(image_embeds)
    text_values, text_inverse, text_unit = unit_rows(text_embeds)
    scale, bias = logit_scale[0], logit_bias[0]
    rows = image_unit.shape[0]
    images = jnp.concatenate([image_unit, partner(image_unit, "grp", 1)])
    texts = [text_unit]
    for _ in range(STEPS - 1):
        texts.append(shifted(texts[-1], "blk", 2))
    image_total = jnp.zeros((2 * rows, image_unit.shape[1]), jnp.float32)
    text_parts = []
    for step in range(STEPS):
        logits = scale * dot_last(texts[step], images) + bias
        sign = jnp.full(logits.shape, -1.0, jnp.float32)
        if step == 0:
            places = lax.broadcasted_iota(jnp.int32, (rows, rows), 0)
            own = jnp.where(places == positives[0][None, :], 1.0, -1.0)
            sign = jnp.concatenate([own, sign[:, rows:]], axis=1)
        coefficient = (-sign * scale * jax.nn.sigmoid(-sign * logits)).astype(jnp.bfloat16)
        text_parts.append(
            jnp.dot(coefficient, images, preferred_element_type=jnp.float32)
        )
        image_total = image_total + dot_first(coefficient, texts[step])
    image_grad = image_total[:rows] + partner(image_total[rows:].astype(jnp.bfloat16), "grp", 1)
    text_total = text_parts[-1]
    for step in range(STEPS - 2, -1, -1):
        text_total = text_parts[step] + shifted(text_total.astype(jnp.bfloat16), "blk", -2)
    return (
        unit_back(image_values, image_inverse, image_grad),
        unit_back(text_values, text_inverse, text_total),
    )


def line_kernel(
    img_ref, txt_ref, pos_ref, scale_ref, bias_ref, img_out, txt_out,
    images, texts, coefs, parts, img_total, back, back_send, img_send, img_recv,
    i_sems, g_send, g_recv, r_send, r_recv, x_send, x_recv,
):
    rows, width = img_ref.shape
    piece = rows // CHUNKS
    last = STEPS - 1
    g = lax.axis_index("grp")
    b = lax.axis_index("blk")
    z = b // 2
    across = {"grp": g + 2 - 4 * ((g // 2) % 2)}
    scale = scale_ref[0]
    bias = bias_ref[0]

    def at(c):
        return pl.ds(pl.multiple_of(c * piece, piece), piece)

    def device(d):
        return {"blk": b + 2 * d}

    def has(d):
        return (z + d >= 0) & (z + d <= last)

    def side(d):
        return (d + 1) // 2

    def gather_copy(d, j, c):
        part = texts.at[j, at(c)]
        return pltpu.make_async_remote_copy(
            part, part, g_send.at[side(d), j, c], g_recv.at[j, c],
            device_id=device(d), device_id_type=MESH)

    def return_copy(d, j, c):
        return pltpu.make_async_remote_copy(
            back_send.at[j, at(c)], back.at[side(d), j, at(c)],
            r_send.at[side(d), j, c], r_recv.at[side(d), j, c],
            device_id=device(d), device_id_type=MESH)

    def image_copy():
        return pltpu.make_async_remote_copy(
            images.at[pl.ds(0, rows)], images.at[pl.ds(rows, rows)], i_sems.at[0], i_sems.at[1],
            device_id=across, device_id_type=MESH)

    def total_copy(c):
        return pltpu.make_async_remote_copy(
            img_send.at[at(c)], img_recv.at[at(c)], x_send.at[c], x_recv.at[c],
            device_id=across, device_id_type=MESH)

    inward = 1 - 2 * (2 * z // STEPS)
    middle = z * (last - z) // (last - 1)
    early = CHUNKS - AHEAD

    def turned(i):
        return (i + early) % CHUNKS

    barrier = pltpu.get_barrier_semaphore()
    pl.semaphore_signal(barrier, inc=1, device_id=across, device_id_type=MESH)
    for d in (1, -1):
        @pl.when(has(d))
        def _():
            pl.semaphore_signal(barrier, inc=1, device_id=device(d), device_id_type=MESH)

    @pl.loop(0, CHUNKS)
    def _(c):
        texts[z, at(c)] = unit_rows(txt_ref[at(c)])[2]

    pl.semaphore_wait(barrier, 2 + middle)

    @pl.when(middle == 0)
    def _():
        @pl.loop(0, CHUNKS)
        def _(c):
            gather_copy(inward, z, c).start()

    @pl.when(middle == 1)
    def _():
        @pl.loop(early, CHUNKS)
        def _(c):
            gather_copy(inward, z, c).start()
            gather_copy(-inward, z, c).start()

    @pl.loop(0, CHUNKS)
    def _(c):
        images[at(c)] = unit_rows(img_ref[at(c)])[2]

    image_copy().start()

    own_images = images[pl.ds(0, rows)]
    own_texts = texts[z]
    logits = scale * dot_last(own_texts, own_images) + bias
    places = lax.broadcasted_iota(jnp.int32, logits.shape, 0)
    sign = jnp.where(places == pos_ref[...], 1.0, -1.0).astype(jnp.float32)
    coefficient = (-sign * scale * jax.nn.sigmoid(-sign * logits)).astype(jnp.bfloat16)
    parts[z] = jnp.dot(coefficient, own_images, preferred_element_type=jnp.float32)
    img_total[pl.ds(0, rows)] = dot_first(coefficient, own_texts)

    def pass_on(d, j, c):
        gather_copy(d, j, c).wait_recv()
        gather_copy(d, j, c).start()

    def meet(j, c):
        both = images[...]
        logits = scale * dot_last(texts[j, at(c)], both) + bias
        coefficient = (scale * jax.nn.sigmoid(logits)).astype(jnp.bfloat16)
        coefs[j, at(c)] = coefficient
        parts[j, at(c)] = jnp.dot(coefficient, both, preferred_element_type=jnp.float32)

    def give_back(d, j, c):
        back_send[j, at(c)] = parts[j, at(c)].astype(jnp.bfloat16)
        return_copy(d, j, c).start()

    def add_back(d, j, c):
        return_copy(d, j, c).wait_recv()
        total = parts[j, at(c)] + back[side(d), j, at(c)].astype(jnp.float32)
        back_send[j, at(c)] = total.astype(jnp.bfloat16)
        return_copy(d, j, c).start()

    def add_images(j):
        img_total[...] += dot_first(coefs[j], texts[j])

    def send_total():
        @pl.loop(0, CHUNKS)
        def _(c):
            theirs = pl.ds(pl.multiple_of(rows + c * piece, piece), piece)
            img_send[at(c)] = img_total[theirs].astype(jnp.bfloat16)
            total_copy(c).start()

    @pl.when(middle == 1)
    def _():
        @pl.loop(0, CHUNKS + LAG)
        def _(i):
            @pl.when(i < CHUNKS)
            def _():
                pass_on(inward, z - inward, i)

            @pl.when(i >= LAG)
            def _():
                pass_on(-inward, z + 2 * inward, i - LAG)

        @pl.loop(0, early)
        def _(c):
            gather_copy(inward, z, c).start()

    image_copy().wait_recv()
    their_images = images[pl.ds(rows, rows)]
    own_texts = texts[z]
    logits = scale * dot_last(own_texts, their_images) + bias
    coefficient = (scale * jax.nn.sigmoid(logits)).astype(jnp.bfloat16)
    parts[z] += jnp.dot(coefficient, their_images, preferred_element_type=jnp.float32)
    img_total[pl.ds(rows, rows)] = dot_first(coefficient, own_texts)

    @pl.when(middle == 0)
    def _():
        @pl.loop(0, (STEPS - 1) * CHUNKS)
        def _(i):
            c = turned(i)
            hops = (last - (i + early) // CHUNKS) % last + 1
            j = z + hops * inward
            gather_copy(-inward, j, c).wait_recv()
            meet(j, c)
            give_back(inward, j, c)

            @pl.when((c == CHUNKS - 1) & (i >= CHUNKS))
            def _():
                add_images(j)

        add_images(z + inward)
        send_total()

    @pl.when(middle == 1)
    def _():
        @pl.loop(0, CHUNKS + HOLD)
        def _(i):
            @pl.when(i < CHUNKS)
            def _():
                pass_on(-inward, z + inward, turned(i))

                @pl.when(i == CHUNKS - 1)
                def _():
                    @pl.loop(0, early)
                    def _(c):
                        gather_copy(-inward, z, c).start()

                meet(z - inward, i)
                meet(z + 2 * inward, i)

            @pl.when(i >= HOLD)
            def _():
                add_back(inward, z + 2 * inward, i - HOLD)
                meet(z + inward, turned(i - HOLD))

        @pl.loop(0, STEPS)
        def _(j):
            @pl.when(j != z)
            def _():
                add_images(j)

        send_total()

        @pl.loop(0, CHUNKS)
        def _(c):
            add_back(inward, z + inward, c)
            add_back(-inward, z - inward, c)

    @pl.loop(0, CHUNKS)
    def _(i):
        c = (i + early * middle) % CHUNKS
        for d in (1, -1):
            @pl.when(has(-d))
            def _():
                return_copy(d, z, c).wait_recv()
                parts[z, at(c)] += back[side(d), z, at(c)].astype(jnp.float32)

        values, inverse, _ = unit_rows(txt_ref[at(c)])
        txt_out[at(c)] = unit_back(values, inverse, parts[z, at(c)])

    @pl.loop(0, CHUNKS)
    def _(c):
        total_copy(c).wait_recv()
        values, inverse, _ = unit_rows(img_ref[at(c)])
        total = img_total[at(c)] + img_recv[at(c)].astype(jnp.float32)
        img_out[at(c)] = unit_back(values, inverse, total)

    image_copy().wait_send()

    @pl.loop(0, CHUNKS)
    def _(c):
        total_copy(c).wait_send()

        @pl.loop(0, STEPS)
        def _(j):
            for d in (1, -1):
                @pl.when(((z - j) * d >= 0) & has(d))
                def _():
                    gather_copy(d, j, c).wait_send()

                @pl.when((j - z) * d > 0)
                def _():
                    return_copy(d, j, c).wait_send()


def line_plan(image_embeds, text_embeds, positives, logit_scale, logit_bias):
    rows, width = image_embeds.shape
    vmem = pl.BlockSpec(memory_space=pltpu.VMEM)
    smem = pl.BlockSpec(memory_space=pltpu.SMEM)
    grad = jax.ShapeDtypeStruct((rows, width), jnp.float32)
    dma = pltpu.SemaphoreType.DMA
    half = functools.partial(pltpu.VMEM, dtype=jnp.bfloat16)
    full = functools.partial(pltpu.VMEM, dtype=jnp.float32)
    return pl.pallas_call(
        line_kernel,
        out_shape=(grad, grad),
        in_specs=[vmem, vmem, vmem, smem, smem],
        out_specs=(vmem, vmem),
        scratch_shapes=[
            half((2 * rows, width)),
            half((STEPS, rows, width)),
            half((STEPS, rows, 2 * rows)),
            full((STEPS, rows, width)),
            full((2 * rows, width)),
            half((2, STEPS, rows, width)),
            half((STEPS, rows, width)),
            half((rows, width)),
            half((rows, width)),
            dma((2,)),
            dma((2, STEPS, CHUNKS)),
            dma((STEPS, CHUNKS)),
            dma((2, STEPS, CHUNKS)),
            dma((2, STEPS, CHUNKS)),
            dma((CHUNKS,)),
            dma((CHUNKS,)),
        ],
        compiler_params=pltpu.CompilerParams(
            collective_id=0, has_side_effects=True, vmem_limit_bytes=48 * 2**20
        ),
        cost_estimate=pl.CostEstimate(
            flops=48 * rows * rows * width, bytes_accessed=12 * rows * width, transcendentals=0
        ),
    )(image_embeds, text_embeds, positives, logit_scale, logit_bias)


def solution(mesh):
    whole_line = mesh.shape["blk"] == 2 * STEPS
    return jax.shard_map(
        line_plan if whole_line else window_plan,
        mesh=mesh,
        in_specs=(
            P(("grp", "blk"), None),
            P(("grp", "blk"), None),
            P(("grp", "blk"), None),
            P(),
            P(),
        ),
        out_specs=(P(("grp", "blk"), None), P(("grp", "blk"), None)),
        check_vma=False,
    )
```

```python
import functools

import jax
import jax.numpy as jnp
from jax import lax
from jax.experimental import pallas as pl
from jax.experimental.pallas import tpu as pltpu
from jax.sharding import PartitionSpec as P

STEPS = 4
CHUNKS = 8
AHEAD_IN = 2
AHEAD_OUT = 5
LAG = 2
HOLD = 5
MESH = pl.DeviceIdType.MESH


def partner(value, axis, distance):
    mask = 2**distance
    pairs = [(source, source ^ mask) for source in range(lax.axis_size(axis))]
    return lax.ppermute(value, axis, pairs)


def shifted(value, axis, steps):
    count = lax.axis_size(axis)
    pairs = [(source, (source + steps) % count) for source in range(count)]
    return lax.ppermute(value, axis, pairs)


def unit_rows(embeds):
    values = embeds.astype(jnp.float32)
    inverse = lax.rsqrt(jnp.sum(values * values, axis=-1, keepdims=True) + 1e-06)
    return (values, inverse, (values * inverse).astype(jnp.bfloat16))


def unit_back(values, inverse, grad_unit):
    projection = jnp.sum(values * grad_unit, axis=-1, keepdims=True)
    return inverse * grad_unit - inverse * inverse * inverse * values * projection


def dot_last(a, b):
    return lax.dot_general(a, b, (((1,), (1,)), ((), ())), preferred_element_type=jnp.float32)


def dot_first(a, b):
    return lax.dot_general(a, b, (((0,), (0,)), ((), ())), preferred_element_type=jnp.float32)


def window_plan(image_embeds, text_embeds, positives, logit_scale, logit_bias):
    image_values, image_inverse, image_unit = unit_rows(image_embeds)
    text_values, text_inverse, text_unit = unit_rows(text_embeds)
    scale, bias = logit_scale[0], logit_bias[0]
    rows = image_unit.shape[0]
    images = jnp.concatenate([image_unit, partner(image_unit, "grp", 1)])
    texts = [text_unit]
    for _ in range(STEPS - 1):
        texts.append(shifted(texts[-1], "blk", 2))
    image_total = jnp.zeros((2 * rows, image_unit.shape[1]), jnp.float32)
    text_parts = []
    for step in range(STEPS):
        logits = scale * dot_last(texts[step], images) + bias
        sign = jnp.full(logits.shape, -1.0, jnp.float32)
        if step == 0:
            places = lax.broadcasted_iota(jnp.int32, (rows, rows), 0)
            own = jnp.where(places == positives[0][None, :], 1.0, -1.0)
            sign = jnp.concatenate([own, sign[:, rows:]], axis=1)
        coefficient = (-sign * scale * jax.nn.sigmoid(-sign * logits)).astype(jnp.bfloat16)
        text_parts.append(
            jnp.dot(coefficient, images, preferred_element_type=jnp.float32)
        )
        image_total = image_total + dot_first(coefficient, texts[step])
    image_grad = image_total[:rows] + partner(image_total[rows:].astype(jnp.bfloat16), "grp", 1)
    text_total = text_parts[-1]
    for step in range(STEPS - 2, -1, -1):
        text_total = text_parts[step] + shifted(text_total.astype(jnp.bfloat16), "blk", -2)
    return (
        unit_back(image_values, image_inverse, image_grad),
        unit_back(text_values, text_inverse, text_total),
    )


def line_kernel(
    img_ref, txt_ref, pos_ref, scale_ref, bias_ref, img_out, txt_out,
    images, texts, coefs, parts, img_total, back, back_send, img_send, img_recv,
    i_sems, g_send, g_recv, r_send, r_recv, x_send, x_recv,
):
    rows, width = img_ref.shape
    piece = rows // CHUNKS
    last = STEPS - 1
    g = lax.axis_index("grp")
    b = lax.axis_index("blk")
    z = b // 2
    across = {"grp": g + 2 - 4 * ((g // 2) % 2)}
    scale = scale_ref[0]
    bias = bias_ref[0]

    def at(c):
        return pl.ds(pl.multiple_of(c * piece, piece), piece)

    def device(d):
        return {"blk": b + 2 * d}

    def has(d):
        return (z + d >= 0) & (z + d <= last)

    def side(d):
        return (d + 1) // 2

    def gather_copy(d, j, c):
        part = texts.at[j, at(c)]
        return pltpu.make_async_remote_copy(
            part, part, g_send.at[side(d), j, c], g_recv.at[j, c],
            device_id=device(d), device_id_type=MESH)

    def return_copy(d, j, c):
        return pltpu.make_async_remote_copy(
            back_send.at[j, at(c)], back.at[side(d), j, at(c)],
            r_send.at[side(d), j, c], r_recv.at[side(d), j, c],
            device_id=device(d), device_id_type=MESH)

    def image_copy():
        return pltpu.make_async_remote_copy(
            images.at[pl.ds(0, rows)], images.at[pl.ds(rows, rows)], i_sems.at[0], i_sems.at[1],
            device_id=across, device_id_type=MESH)

    def total_copy(c):
        return pltpu.make_async_remote_copy(
            img_send.at[at(c)], img_recv.at[at(c)], x_send.at[c], x_recv.at[c],
            device_id=across, device_id_type=MESH)

    inward = 1 - 2 * (2 * z // STEPS)
    middle = z * (last - z) // (last - 1)
    early = CHUNKS - AHEAD_IN
    early_out = CHUNKS - AHEAD_OUT

    barrier = pltpu.get_barrier_semaphore()
    pl.semaphore_signal(barrier, inc=1, device_id=across, device_id_type=MESH)
    for d in (1, -1):
        @pl.when(has(d))
        def _():
            pl.semaphore_signal(barrier, inc=1, device_id=device(d), device_id_type=MESH)

    @pl.loop(0, CHUNKS)
    def _(c):
        images[at(c)] = unit_rows(img_ref[at(c)])[2]
        texts[z, at(c)] = unit_rows(txt_ref[at(c)])[2]

    pl.semaphore_wait(barrier, 2 + middle)
    image_copy().start()

    @pl.when(middle == 0)
    def _():
        @pl.loop(0, CHUNKS)
        def _(c):
            gather_copy(inward, z, c).start()

    @pl.when(middle == 1)
    def _():
        @pl.loop(early, CHUNKS)
        def _(c):
            gather_copy(inward, z, c).start()

        @pl.loop(early_out, CHUNKS)
        def _(c):
            gather_copy(-inward, z, c).start()

    own_images = images[pl.ds(0, rows)]
    own_texts = texts[z]
    logits = scale * dot_last(own_texts, own_images) + bias
    places = lax.broadcasted_iota(jnp.int32, logits.shape, 0)
    sign = jnp.where(places == pos_ref[...], 1.0, -1.0).astype(jnp.float32)
    coefficient = (-sign * scale * jax.nn.sigmoid(-sign * logits)).astype(jnp.bfloat16)
    parts[z] = jnp.dot(coefficient, own_images, preferred_element_type=jnp.float32)
    img_total[pl.ds(0, rows)] = dot_first(coefficient, own_texts)

    def pass_on(d, j, c):
        gather_copy(d, j, c).wait_recv()
        gather_copy(d, j, c).start()

    def meet(j, c):
        both = images[...]
        logits = scale * dot_last(texts[j, at(c)], both) + bias
        coefficient = (scale * jax.nn.sigmoid(logits)).astype(jnp.bfloat16)
        coefs[j, at(c)] = coefficient
        parts[j, at(c)] = jnp.dot(coefficient, both, preferred_element_type=jnp.float32)

    def give_back(d, j, c):
        back_send[j, at(c)] = parts[j, at(c)].astype(jnp.bfloat16)
        return_copy(d, j, c).start()

    def add_back(d, j, c):
        return_copy(d, j, c).wait_recv()
        total = parts[j, at(c)] + back[side(d), j, at(c)].astype(jnp.float32)
        back_send[j, at(c)] = total.astype(jnp.bfloat16)
        return_copy(d, j, c).start()

    def add_images(j):
        img_total[...] += dot_first(coefs[j], texts[j])

    def send_total():
        @pl.loop(0, CHUNKS)
        def _(c):
            theirs = pl.ds(pl.multiple_of(rows + c * piece, piece), piece)
            img_send[at(c)] = img_total[theirs].astype(jnp.bfloat16)
            total_copy(c).start()

    @pl.when(middle == 1)
    def _():
        @pl.loop(0, CHUNKS + LAG)
        def _(i):
            @pl.when(i < CHUNKS)
            def _():
                pass_on(inward, z - inward, i)

            @pl.when(i >= LAG)
            def _():
                pass_on(-inward, z + 2 * inward, i - LAG)

        @pl.loop(0, early)
        def _(c):
            gather_copy(inward, z, c).start()

    image_copy().wait_recv()
    def meet_theirs():
        their_images = images[pl.ds(rows, rows)]
        own_texts = texts[z]
        logits = scale * dot_last(own_texts, their_images) + bias
        coefficient = (scale * jax.nn.sigmoid(logits)).astype(jnp.bfloat16)
        parts[z] += jnp.dot(coefficient, their_images, preferred_element_type=jnp.float32)
        img_total[pl.ds(rows, rows)] = dot_first(coefficient, own_texts)

    @pl.when(middle == 0)
    def _():
        @pl.loop(0, (STEPS - 1) * CHUNKS)
        def _(i):
            c = (i + early_out) % CHUNKS
            hops = (last - (i + early_out) // CHUNKS) % last + 1
            j = z + hops * inward
            gather_copy(-inward, j, c).wait_recv()
            meet(j, c)
            give_back(inward, j, c)

            @pl.when(i == AHEAD_OUT)
            def _():
                meet_theirs()

            @pl.when((c == CHUNKS - 1) & (i >= CHUNKS))
            def _():
                add_images(j)

        add_images(z + inward)
        send_total()

    @pl.when(middle == 1)
    def _():
        meet_theirs()

        @pl.loop(0, CHUNKS + HOLD)
        def _(i):
            @pl.when(i < CHUNKS)
            def _():
                pass_on(-inward, z + inward, (i + early) % CHUNKS)

                @pl.when(i == CHUNKS - 1)
                def _():
                    @pl.loop(0, early_out)
                    def _(c):
                        gather_copy(-inward, z, c).start()

                meet(z - inward, i)
                meet(z + 2 * inward, i)

            @pl.when(i >= HOLD)
            def _():
                add_back(inward, z + 2 * inward, i - HOLD)
                meet(z + inward, (i - HOLD + early) % CHUNKS)

        @pl.loop(0, STEPS)
        def _(j):
            @pl.when(j != z)
            def _():
                add_images(j)

        send_total()

        @pl.loop(0, CHUNKS)
        def _(c):
            add_back(inward, z + inward, c)
            add_back(-inward, z - inward, c)

    @pl.loop(0, CHUNKS)
    def _(i):
        c = (i + early_out * middle) % CHUNKS
        for d in (1, -1):
            @pl.when(has(-d))
            def _():
                return_copy(d, z, c).wait_recv()
                parts[z, at(c)] += back[side(d), z, at(c)].astype(jnp.float32)

        values, inverse, _ = unit_rows(txt_ref[at(c)])
        txt_out[at(c)] = unit_back(values, inverse, parts[z, at(c)])

    @pl.loop(0, CHUNKS)
    def _(c):
        total_copy(c).wait_recv()
        values, inverse, _ = unit_rows(img_ref[at(c)])
        total = img_total[at(c)] + img_recv[at(c)].astype(jnp.float32)
        img_out[at(c)] = unit_back(values, inverse, total)

    image_copy().wait_send()

    @pl.loop(0, CHUNKS)
    def _(c):
        total_copy(c).wait_send()

        @pl.loop(0, STEPS)
        def _(j):
            for d in (1, -1):
                @pl.when(((z - j) * d >= 0) & has(d))
                def _():
                    gather_copy(d, j, c).wait_send()

                @pl.when((j - z) * d > 0)
                def _():
                    return_copy(d, j, c).wait_send()


def line_plan(image_embeds, text_embeds, positives, logit_scale, logit_bias):
    rows, width = image_embeds.shape
    vmem = pl.BlockSpec(memory_space=pltpu.VMEM)
    smem = pl.BlockSpec(memory_space=pltpu.SMEM)
    grad = jax.ShapeDtypeStruct((rows, width), jnp.float32)
    dma = pltpu.SemaphoreType.DMA
    half = functools.partial(pltpu.VMEM, dtype=jnp.bfloat16)
    full = functools.partial(pltpu.VMEM, dtype=jnp.float32)
    return pl.pallas_call(
        line_kernel,
        out_shape=(grad, grad),
        in_specs=[vmem, vmem, vmem, smem, smem],
        out_specs=(vmem, vmem),
        scratch_shapes=[
            half((2 * rows, width)),
            half((STEPS, rows, width)),
            half((STEPS, rows, 2 * rows)),
            full((STEPS, rows, width)),
            full((2 * rows, width)),
            half((2, STEPS, rows, width)),
            half((STEPS, rows, width)),
            half((rows, width)),
            half((rows, width)),
            dma((2,)),
            dma((2, STEPS, CHUNKS)),
            dma((STEPS, CHUNKS)),
            dma((2, STEPS, CHUNKS)),
            dma((2, STEPS, CHUNKS)),
            dma((CHUNKS,)),
            dma((CHUNKS,)),
        ],
        compiler_params=pltpu.CompilerParams(
            collective_id=0, has_side_effects=True, vmem_limit_bytes=48 * 2**20
        ),
        cost_estimate=pl.CostEstimate(
            flops=48 * rows * rows * width, bytes_accessed=12 * rows * width, transcendentals=0
        ),
    )(image_embeds, text_embeds, positives, logit_scale, logit_bias)


def solution(mesh):
    whole_line = mesh.shape["blk"] == 2 * STEPS
    return jax.shard_map(
        line_plan if whole_line else window_plan,
        mesh=mesh,
        in_specs=(
            P(("grp", "blk"), None),
            P(("grp", "blk"), None),
            P(("grp", "blk"), None),
            P(),
            P(),
        ),
        out_specs=(P(("grp", "blk"), None), P(("grp", "blk"), None)),
        check_vma=False,
    )
```

```python
import functools

import jax
import jax.numpy as jnp
from jax import lax
from jax.experimental import pallas as pl
from jax.experimental.pallas import tpu as pltpu
from jax.sharding import PartitionSpec as P

STEPS = 4
CHUNKS = 8
AHEAD_IN = 2
AHEAD_OUT = 5
LAG = 2
HOLD = 5
MESH = pl.DeviceIdType.MESH


def partner(value, axis, distance):
    mask = 2**distance
    pairs = [(source, source ^ mask) for source in range(lax.axis_size(axis))]
    return lax.ppermute(value, axis, pairs)


def shifted(value, axis, steps):
    count = lax.axis_size(axis)
    pairs = [(source, (source + steps) % count) for source in range(count)]
    return lax.ppermute(value, axis, pairs)


def unit_rows(embeds):
    values = embeds.astype(jnp.float32)
    inverse = lax.rsqrt(jnp.sum(values * values, axis=-1, keepdims=True) + 1e-06)
    return (values, inverse, (values * inverse).astype(jnp.bfloat16))


def unit_back(values, inverse, grad_unit):
    projection = jnp.sum(values * grad_unit, axis=-1, keepdims=True)
    return inverse * grad_unit - inverse * inverse * inverse * values * projection


def dot_last(a, b):
    return lax.dot_general(a, b, (((1,), (1,)), ((), ())), preferred_element_type=jnp.float32)


def dot_first(a, b):
    return lax.dot_general(a, b, (((0,), (0,)), ((), ())), preferred_element_type=jnp.float32)


def window_plan(image_embeds, text_embeds, positives, logit_scale, logit_bias):
    image_values, image_inverse, image_unit = unit_rows(image_embeds)
    text_values, text_inverse, text_unit = unit_rows(text_embeds)
    scale, bias = logit_scale[0], logit_bias[0]
    rows = image_unit.shape[0]
    images = jnp.concatenate([image_unit, partner(image_unit, "grp", 1)])
    texts = [text_unit]
    for _ in range(STEPS - 1):
        texts.append(shifted(texts[-1], "blk", 2))
    image_total = jnp.zeros((2 * rows, image_unit.shape[1]), jnp.float32)
    text_parts = []
    for step in range(STEPS):
        logits = scale * dot_last(texts[step], images) + bias
        sign = jnp.full(logits.shape, -1.0, jnp.float32)
        if step == 0:
            places = lax.broadcasted_iota(jnp.int32, (rows, rows), 0)
            own = jnp.where(places == positives[0][None, :], 1.0, -1.0)
            sign = jnp.concatenate([own, sign[:, rows:]], axis=1)
        coefficient = (-sign * scale * jax.nn.sigmoid(-sign * logits)).astype(jnp.bfloat16)
        text_parts.append(
            jnp.dot(coefficient, images, preferred_element_type=jnp.float32)
        )
        image_total = image_total + dot_first(coefficient, texts[step])
    image_grad = image_total[:rows] + partner(image_total[rows:].astype(jnp.bfloat16), "grp", 1)
    text_total = text_parts[-1]
    for step in range(STEPS - 2, -1, -1):
        text_total = text_parts[step] + shifted(text_total.astype(jnp.bfloat16), "blk", -2)
    return (
        unit_back(image_values, image_inverse, image_grad),
        unit_back(text_values, text_inverse, text_total),
    )


def line_kernel(
    img_ref, txt_ref, pos_ref, scale_ref, bias_ref, img_out, txt_out,
    images, texts, coefs, parts, img_total, back, back_send, img_send, img_recv,
    i_sems, g_send, g_recv, r_send, r_recv, x_send, x_recv,
):
    rows, width = img_ref.shape
    piece = rows // CHUNKS
    last = STEPS - 1
    g = lax.axis_index("grp")
    b = lax.axis_index("blk")
    z = b // 2
    across = {"grp": g + 2 - 4 * ((g // 2) % 2)}
    scale = scale_ref[0]
    bias = bias_ref[0]

    def at(c):
        return pl.ds(pl.multiple_of(c * piece, piece), piece)

    def device(d):
        return {"blk": b + 2 * d}

    def has(d):
        return (z + d >= 0) & (z + d <= last)

    def side(d):
        return (d + 1) // 2

    def gather_copy(d, j, c):
        part = texts.at[j, at(c)]
        return pltpu.make_async_remote_copy(
            part, part, g_send.at[side(d), j, c], g_recv.at[j, c],
            device_id=device(d), device_id_type=MESH)

    def return_copy(d, j, c):
        return pltpu.make_async_remote_copy(
            back_send.at[j, at(c)], back.at[side(d), j, at(c)],
            r_send.at[side(d), j, c], r_recv.at[side(d), j, c],
            device_id=device(d), device_id_type=MESH)

    def image_copy():
        return pltpu.make_async_remote_copy(
            images.at[pl.ds(0, rows)], images.at[pl.ds(rows, rows)], i_sems.at[0], i_sems.at[1],
            device_id=across, device_id_type=MESH)

    def total_copy(c):
        return pltpu.make_async_remote_copy(
            img_send.at[at(c)], img_recv.at[at(c)], x_send.at[c], x_recv.at[c],
            device_id=across, device_id_type=MESH)

    inward = 1 - 2 * (2 * z // STEPS)
    middle = z * (last - z) // (last - 1)
    early = CHUNKS - AHEAD_IN
    early_out = CHUNKS - AHEAD_OUT

    barrier = pltpu.get_barrier_semaphore()
    pl.semaphore_signal(barrier, inc=1, device_id=across, device_id_type=MESH)
    for d in (1, -1):
        @pl.when(has(d))
        def _():
            pl.semaphore_signal(barrier, inc=1, device_id=device(d), device_id_type=MESH)

    @pl.loop(0, 2)
    def _(i):
        half = pl.ds(pl.multiple_of(i * (rows // 2), rows // 2), rows // 2)
        images[half] = unit_rows(img_ref[half])[2]
        texts[z, half] = unit_rows(txt_ref[half])[2]

    pl.semaphore_wait(barrier, 2 + middle)
    image_copy().start()

    @pl.when(middle == 0)
    def _():
        @pl.loop(0, CHUNKS)
        def _(c):
            gather_copy(inward, z, c).start()

    @pl.when(middle == 1)
    def _():
        @pl.loop(early, CHUNKS)
        def _(c):
            gather_copy(inward, z, c).start()

        @pl.loop(early_out, CHUNKS)
        def _(c):
            gather_copy(-inward, z, c).start()

    own_images = images[pl.ds(0, rows)]
    own_texts = texts[z]
    logits = scale * dot_last(own_texts, own_images) + bias
    places = lax.broadcasted_iota(jnp.int32, logits.shape, 0)
    sign = jnp.where(places == pos_ref[...], 1.0, -1.0).astype(jnp.float32)
    coefficient = (-sign * scale * jax.nn.sigmoid(-sign * logits)).astype(jnp.bfloat16)
    parts[z] = jnp.dot(coefficient, own_images, preferred_element_type=jnp.float32)
    img_total[pl.ds(0, rows)] = dot_first(coefficient, own_texts)

    def pass_on(d, j, c):
        gather_copy(d, j, c).wait_recv()
        gather_copy(d, j, c).start()

    def meet(j, c):
        both = images[...]
        logits = scale * dot_last(texts[j, at(c)], both) + bias
        coefficient = (scale * jax.nn.sigmoid(logits)).astype(jnp.bfloat16)
        coefs[j, at(c)] = coefficient
        parts[j, at(c)] = jnp.dot(coefficient, both, preferred_element_type=jnp.float32)

    def give_back(d, j, c):
        back_send[j, at(c)] = parts[j, at(c)].astype(jnp.bfloat16)
        return_copy(d, j, c).start()

    def add_back(d, j, c):
        return_copy(d, j, c).wait_recv()
        total = parts[j, at(c)] + back[side(d), j, at(c)].astype(jnp.float32)
        back_send[j, at(c)] = total.astype(jnp.bfloat16)
        return_copy(d, j, c).start()

    def add_images(j):
        img_total[...] += dot_first(coefs[j], texts[j])

    def send_total():
        @pl.loop(0, CHUNKS)
        def _(c):
            theirs = pl.ds(pl.multiple_of(rows + c * piece, piece), piece)
            img_send[at(c)] = img_total[theirs].astype(jnp.bfloat16)
            total_copy(c).start()

    @pl.when(middle == 1)
    def _():
        @pl.loop(0, CHUNKS + LAG)
        def _(i):
            @pl.when(i < CHUNKS)
            def _():
                pass_on(inward, z - inward, i)

            @pl.when(i >= LAG)
            def _():
                pass_on(-inward, z + 2 * inward, i - LAG)

        @pl.loop(0, early)
        def _(c):
            gather_copy(inward, z, c).start()

    image_copy().wait_recv()
    def meet_theirs():
        their_images = images[pl.ds(rows, rows)]
        own_texts = texts[z]
        logits = scale * dot_last(own_texts, their_images) + bias
        coefficient = (scale * jax.nn.sigmoid(logits)).astype(jnp.bfloat16)
        parts[z] += jnp.dot(coefficient, their_images, preferred_element_type=jnp.float32)
        img_total[pl.ds(rows, rows)] = dot_first(coefficient, own_texts)

    @pl.when(middle == 0)
    def _():
        @pl.loop(0, (STEPS - 1) * CHUNKS)
        def _(i):
            c = (i + early_out) % CHUNKS
            hops = (last - (i + early_out) // CHUNKS) % last + 1
            j = z + hops * inward
            gather_copy(-inward, j, c).wait_recv()
            meet(j, c)
            give_back(inward, j, c)

            @pl.when(i == AHEAD_OUT)
            def _():
                meet_theirs()

            @pl.when((c == CHUNKS - 1) & (i >= CHUNKS))
            def _():
                add_images(j)

        add_images(z + inward)
        send_total()

    @pl.when(middle == 1)
    def _():
        meet_theirs()

        @pl.loop(0, CHUNKS + HOLD)
        def _(i):
            @pl.when(i < CHUNKS)
            def _():
                pass_on(-inward, z + inward, (i + early) % CHUNKS)

                @pl.when(i == CHUNKS - 1)
                def _():
                    @pl.loop(0, early_out)
                    def _(c):
                        gather_copy(-inward, z, c).start()

                meet(z - inward, i)
                meet(z + 2 * inward, i)

            @pl.when(i >= HOLD)
            def _():
                add_back(inward, z + 2 * inward, i - HOLD)
                meet(z + inward, (i - HOLD + early) % CHUNKS)

            @pl.when(i >= HOLD + LAG)
            def _():
                add_back(-inward, z - inward, i - HOLD - LAG)

            @pl.when((i == CHUNKS) | (i == CHUNKS + 2))
            def _():
                add_images(z - inward + (i - CHUNKS) // 2 * 3 * inward)

        add_images(z + inward)
        send_total()

        @pl.loop(0, CHUNKS)
        def _(c):
            add_back(inward, z + inward, c)

            @pl.when(c < LAG)
            def _():
                add_back(-inward, z - inward, CHUNKS - LAG + c)

    @pl.loop(0, CHUNKS)
    def _(i):
        c = (i + early_out * middle) % CHUNKS
        for d in (1, -1):
            @pl.when(has(-d))
            def _():
                return_copy(d, z, c).wait_recv()
                parts[z, at(c)] += back[side(d), z, at(c)].astype(jnp.float32)

        values, inverse, _ = unit_rows(txt_ref[at(c)])
        txt_out[at(c)] = unit_back(values, inverse, parts[z, at(c)])

        total_copy(i).wait_recv()
        values, inverse, _ = unit_rows(img_ref[at(i)])
        total = img_total[at(i)] + img_recv[at(i)].astype(jnp.float32)
        img_out[at(i)] = unit_back(values, inverse, total)

    image_copy().wait_send()

    @pl.loop(0, CHUNKS)
    def _(c):
        total_copy(c).wait_send()

        @pl.loop(0, STEPS)
        def _(j):
            for d in (1, -1):
                @pl.when(((z - j) * d >= 0) & has(d))
                def _():
                    gather_copy(d, j, c).wait_send()

                @pl.when((j - z) * d > 0)
                def _():
                    return_copy(d, j, c).wait_send()


def line_plan(image_embeds, text_embeds, positives, logit_scale, logit_bias):
    rows, width = image_embeds.shape
    vmem = pl.BlockSpec(memory_space=pltpu.VMEM)
    smem = pl.BlockSpec(memory_space=pltpu.SMEM)
    grad = jax.ShapeDtypeStruct((rows, width), jnp.float32)
    dma = pltpu.SemaphoreType.DMA
    half = functools.partial(pltpu.VMEM, dtype=jnp.bfloat16)
    full = functools.partial(pltpu.VMEM, dtype=jnp.float32)
    return pl.pallas_call(
        line_kernel,
        out_shape=(grad, grad),
        in_specs=[vmem, vmem, vmem, smem, smem],
        out_specs=(vmem, vmem),
        scratch_shapes=[
            half((2 * rows, width)),
            half((STEPS, rows, width)),
            half((STEPS, rows, 2 * rows)),
            full((STEPS, rows, width)),
            full((2 * rows, width)),
            half((2, STEPS, rows, width)),
            half((STEPS, rows, width)),
            half((rows, width)),
            half((rows, width)),
            dma((2,)),
            dma((2, STEPS, CHUNKS)),
            dma((STEPS, CHUNKS)),
            dma((2, STEPS, CHUNKS)),
            dma((2, STEPS, CHUNKS)),
            dma((CHUNKS,)),
            dma((CHUNKS,)),
        ],
        compiler_params=pltpu.CompilerParams(
            collective_id=0, has_side_effects=True, vmem_limit_bytes=48 * 2**20
        ),
        cost_estimate=pl.CostEstimate(
            flops=48 * rows * rows * width, bytes_accessed=12 * rows * width, transcendentals=0
        ),
    )(image_embeds, text_embeds, positives, logit_scale, logit_bias)


def solution(mesh):
    whole_line = mesh.shape["blk"] == 2 * STEPS
    return jax.shard_map(
        line_plan if whole_line else window_plan,
        mesh=mesh,
        in_specs=(
            P(("grp", "blk"), None),
            P(("grp", "blk"), None),
            P(("grp", "blk"), None),
            P(),
            P(),
        ),
        out_specs=(P(("grp", "blk"), None), P(("grp", "blk"), None)),
        check_vma=False,
    )
```
